512 devices in a mesh: section: 32 (over x, z_lo, core), tp: 16 (over y, z_hi).
Axes of the slice: x: 4, y: 4, z: 16 (z_hi: 4, z_lo: 4; z = z_hi * 4 + z_lo), core: 2. Of those that a mesh axis runs over, the one named last changes fastest.
Arguments:
- held_query: bfloat16 [32, 1024, 64, 128], P('section', 'tp'), may hold values from -6 to 6
- held_key: bfloat16 [32, 1024, 16, 128], P('section', None, 'tp'), may hold values from -6 to 6
- held_value: bfloat16 [32, 1024, 16, 128], P('section', None, 'tp'), may hold values from -6 to 6
- grad_out: bfloat16 [32, 1024, 64, 128], P('section', None, 'tp'), may hold values from -6 to 6
Outputs:
- grad_query: bfloat16 [32, 1024, 64, 128], P('section', None, 'tp')
- grad_key: bfloat16 [32, 1024, 16, 128], P('section', None, 'tp')
- grad_value: bfloat16 [32, 1024, 16, 128], P('section', None, 'tp')
The draws below stay inside these ranges and needn't reach their ends.
All inputs are finite; a program needn't handle non-finite values.
Results may differ from the reference program's by a relative error of at most 0.0064.
Values may be sent and summed in bfloat16 or wider, within the bound.
A program may use at most 64 MiB of HBM per device.

```python
import jax
import jax.numpy as jnp
from jax import lax

HQ = 64
HD = 128
SEQ = 1024
SECTIONS = 32
KV_HELD = 16


def draw_held_query(key, part):
    key = jax.random.fold_in(key, 1)
    base = jnp.clip(jax.random.normal(key, (SECTIONS, SEQ, HQ, HD), jnp.float32), -6.0, 6.0)
    return base.astype(jnp.bfloat16)


def draw_held_key(key, part):
    key = jax.random.fold_in(key, 2)
    base = jnp.clip(jax.random.normal(key, (SECTIONS, SEQ, KV_HELD, HD), jnp.float32), -6.0, 6.0)
    return base.astype(jnp.bfloat16)


def block_scale(stream_key, dims, cuts, least, largest):
    level = 1.0
    for axis_at, shards_of in cuts:
        steps = jax.random.uniform(jax.random.fold_in(jax.random.fold_in(stream_key, 6), axis_at), (shards_of,), jnp.float32, least / len(cuts), largest / len(cuts))
        level = level * jnp.repeat(jnp.exp(steps), dims[axis_at] // shards_of).reshape((-1,) + (1,) * (len(dims) - 1 - axis_at))
    return level


def scatter_about(own_key, shape, scale, limit, pieces=(), held_as=jnp.bfloat16):
    level = block_scale(own_key, shape, pieces, -0.22, 0.18) if pieces else 1.0
    values = jax.random.normal(own_key, shape, jnp.float32) * scale * level
    return jnp.minimum(jnp.maximum(values, -limit), limit).astype(held_as)


def setup_inputs(seed: int = 0) -> dict:
    streams_of = jax.random.split(jax.random.key(seed), 5)
    return {
        "held_query": draw_held_query(jax.random.fold_in(streams_of[4], 71), 0),
        "held_key": draw_held_key(jax.random.fold_in(streams_of[4], 71), 0),
        "held_value": scatter_about(streams_of[2], (SECTIONS, SEQ, KV_HELD, HD), 1.0, 6.0, ((0, 32), (2, 16))),
        "grad_out": scatter_about(streams_of[3], (SECTIONS, SEQ, HQ, HD), 1.0, 6.0, ((0, 32), (2, 16))),
    }


def head_backward(query, key, value, upstream):
    width = query.shape[-1]
    scale = width ** -0.5
    length = query.shape[0]
    scores = lax.dot_general(query, key, (((1,), (1,)), ((), ())), preferred_element_type=jnp.float32) * scale
    later = lax.broadcasted_iota(jnp.int32, (length, length), 0) >= lax.broadcasted_iota(jnp.int32, (length, length), 1)
    scores = jnp.where(later, scores, -1e30)
    top = jnp.max(scores, axis=1, keepdims=True)
    weights = jnp.exp(scores - top)
    probs = weights / jnp.sum(weights, axis=1, keepdims=True)
    probs_low = probs.astype(jnp.bfloat16)
    grad_value = lax.dot_general(probs_low, upstream, (((0,), (0,)), ((), ())), preferred_element_type=jnp.float32)
    grad_probs = lax.dot_general(upstream, value, (((1,), (1,)), ((), ())), preferred_element_type=jnp.float32)
    delta = jnp.sum(probs * grad_probs, axis=1, keepdims=True)
    grad_scores = (probs * (grad_probs - delta) * scale).astype(jnp.bfloat16)
    grad_query = jnp.dot(grad_scores, key, preferred_element_type=jnp.float32)
    grad_key = lax.dot_general(grad_scores, query, (((0,), (0,)), ((), ())), preferred_element_type=jnp.float32)
    return grad_query, grad_key, grad_value


def slot_backward(query, key, value, upstream):
    heads = query.shape[1]
    slots = key.shape[1]
    group = heads // slots
    length = query.shape[0]
    width = query.shape[2]
    key_rep = jnp.repeat(key, group, axis=1)
    value_rep = jnp.repeat(value, group, axis=1)
    stacked = (jnp.moveaxis(query, 1, 0), jnp.moveaxis(key_rep, 1, 0), jnp.moveaxis(value_rep, 1, 0), jnp.moveaxis(upstream, 1, 0))

    def one_head(items):
        return head_backward(items[0], items[1], items[2], items[3])

    head_query, head_key, head_value = lax.map(one_head, stacked)
    grad_query = jnp.moveaxis(head_query, 0, 1).astype(jnp.bfloat16)
    grad_key = jnp.sum(head_key.reshape(slots, group, length, width), axis=1)
    grad_value = jnp.sum(head_value.reshape(slots, group, length, width), axis=1)
    return grad_query, jnp.moveaxis(grad_key, 0, 1).astype(jnp.bfloat16), jnp.moveaxis(grad_value, 0, 1).astype(jnp.bfloat16)


def reference(held_query, held_key, held_value, grad_out):
    stash = (held_query[::-1], held_key[::-1], held_value[::-1], grad_out)

    def one_section(items):
        return slot_backward(items[0], items[1], items[2], items[3])

    grad_q, grad_k, grad_v = lax.map(one_section, stash)

    def upward(array):
        return jnp.concatenate([array[1:], jnp.zeros_like(array[:1])], axis=0)

    return upward(grad_q), upward(grad_k), upward(grad_v)
```

```python
import functools

import jax
import jax.numpy as jnp
from jax import lax
from jax.experimental import pallas as pl
from jax.experimental.pallas import tpu as pltpu
from jax.sharding import PartitionSpec as P

MESH = pl.DeviceIdType.MESH
LOG2E = 1.4426950408889634
CONTRACT_LAST = (((1,), (1,)), ((), ()))


def local_wait(ref, sem):
    pltpu.make_async_copy(ref, ref, sem).wait()


def kernel(
    sections, parts, tokens, group,
    q_ref, k_ref, v_ref, g_ref,
    dq_ref, dk_ref, dv_ref,
    q_in, k_in, v_in, g_in, k_turned, dk_sum, dv_sum,
    q_sem, g_sem, k_sem, v_sem, q_out_sem, g_out_sem, k_out_sem, v_out_sem,
):
    s = lax.axis_index("section")
    t = lax.axis_index("tp")
    rows = tokens * group
    length = parts * tokens
    width = q_ref.shape[-1]
    scale = width ** (-0.5)
    works = s < sections - 1
    partner = sections - 2 - s
    alone = partner == s
    gives = s > 0

    def at_step(step):
        return lax.rem(5 * step + s, parts)

    def block(index):
        return pl.ds(pl.multiple_of(index * rows, rows), rows)

    barrier = pltpu.get_barrier_semaphore()

    def greet(index, carry):
        @pl.when(jnp.logical_and(works, jnp.logical_not(jnp.logical_and(alone, index == t))))
        def _():
            pl.semaphore_signal(barrier, inc=1, device_id=(partner, index), device_id_type=MESH)
        return carry

    lax.fori_loop(0, parts, greet, 0)

    @pl.when(works)
    def _():
        pl.semaphore_signal(barrier, inc=1, device_id=(s + 1, t), device_id_type=MESH)

    pl.semaphore_wait(
        barrier,
        jnp.where(works, parts, 0) - jnp.where(alone, 1, 0) + jnp.where(gives, 1, 0),
    )

    def hand_over(source, target, out_sem, in_sem):
        @pl.when(jnp.logical_and(works, jnp.logical_not(alone)))
        def _():
            pltpu.make_async_remote_copy(
                src_ref=source, dst_ref=target, send_sem=out_sem, recv_sem=in_sem,
                device_id=(partner, t), device_id_type=MESH,
            ).start()

        @pl.when(alone)
        def _():
            pltpu.make_async_copy(source, target, in_sem).start()

    hand_over(k_ref, k_in, k_out_sem, k_sem)
    hand_over(v_ref, v_in, v_out_sem, v_sem)

    def send(step, carry):
        @pl.when(gives)
        def _():
            theirs = lax.rem(lax.rem(5 * step + s - 1, parts) + t, parts)
            pltpu.make_async_remote_copy(
                src_ref=g_ref.at[block(theirs)],
                dst_ref=g_in.at[block(theirs)],
                send_sem=g_out_sem,
                recv_sem=g_sem.at[theirs],
                device_id=(s - 1, t),
                device_id_type=MESH,
            ).start()

        @pl.when(works)
        def _():
            shift = lax.rem(5 * step + partner, parts)
            to = lax.rem(t + parts - shift, parts)
            itself = jnp.logical_and(alone, to == t)

            @pl.when(jnp.logical_not(itself))
            def _():
                pltpu.make_async_remote_copy(
                    src_ref=q_ref.at[block(to)],
                    dst_ref=q_in.at[block(t)],
                    send_sem=q_out_sem,
                    recv_sem=q_sem.at[t],
                    device_id=(partner, to),
                    device_id_type=MESH,
                ).start()

            @pl.when(itself)
            def _():
                pltpu.make_async_copy(q_ref.at[block(to)], q_in.at[block(t)], q_sem.at[t]).start()

        return carry

    lax.fori_loop(0, parts, send, 0)

    dk_sum[...] = jnp.zeros_like(dk_sum)
    dv_sum[...] = jnp.zeros_like(dv_sum)

    def backward(index, keys):
        here = block(index)
        query, upstream = q_in[here, :], g_in[here, :]
        key, value = k_in[:keys, :], v_in[:keys, :]
        scores = lax.dot_general(key, query, CONTRACT_LAST, preferred_element_type=jnp.float32)
        token = index * tokens + lax.broadcasted_iota(jnp.int32, (keys, rows), 1) // group
        seen = lax.broadcasted_iota(jnp.int32, (keys, rows), 0) <= token
        scores = jnp.where(seen, scores, -1e30)
        top = jnp.max(scores, axis=0, keepdims=True)
        weights = jnp.exp2((scores - top) * (scale * LOG2E))
        share = 1.0 / jnp.sum(weights, axis=0, keepdims=True)
        probs = weights * share
        dv_sum[:keys, :] += jnp.dot(
            probs.astype(jnp.bfloat16), upstream, preferred_element_type=jnp.float32
        )
        grad_probs = lax.dot_general(
            value, upstream, CONTRACT_LAST, preferred_element_type=jnp.float32
        )
        delta = jnp.sum(probs * grad_probs, axis=0, keepdims=True)
        grad_scores = (probs * (grad_probs - delta) * scale).astype(jnp.bfloat16)
        dk_sum[:keys, :] += jnp.dot(grad_scores, query, preferred_element_type=jnp.float32)
        turned = jnp.dot(k_turned[:, :keys], grad_scores, preferred_element_type=jnp.float32)
        dq_ref[here, :] = turned.T.astype(dq_ref.dtype)

    @pl.when(works)
    def _():
        local_wait(k_in, k_sem)
        local_wait(v_in, v_sem)
        k_turned[...] = k_in[...].T

        def take(step, carry):
            index = lax.rem(at_step(step) + t, parts)
            local_wait(q_in.at[block(index)], q_sem.at[index])
            local_wait(g_in.at[block(index)], g_sem.at[index])
            spans = 4
            for span in range(spans):
                @pl.when(index // (parts // spans) == span)
                def _():
                    backward(index, (span + 1) * length // spans)
            return carry

        lax.fori_loop(0, parts, take, 0)

    @pl.when(jnp.logical_not(works))
    def _():
        dq_ref[...] = jnp.zeros_like(dq_ref)

    dk_ref[...] = dk_sum[...].astype(dk_ref.dtype)
    dv_ref[...] = dv_sum[...].astype(dv_ref.dtype)

    @pl.when(jnp.logical_and(works, jnp.logical_not(alone)))
    def _():
        local_wait(k_ref, k_out_sem)
        local_wait(v_ref, v_out_sem)
        local_wait(q_ref, q_out_sem)

    @pl.when(alone)
    def _():
        local_wait(q_ref.at[pl.ds(0, (parts - 1) * rows)], q_out_sem)

    @pl.when(gives)
    def _():
        local_wait(g_ref, g_out_sem)


def local(held_query, held_key, held_value, grad_out):
    sections, parts = lax.axis_size("section"), lax.axis_size("tp")
    _, tokens, heads, width = held_query.shape
    length = held_key.shape[1]
    group = heads // parts
    query = held_query.reshape(tokens, parts, group, width)
    query = jnp.swapaxes(query, 0, 1).reshape(parts * tokens * group, width)
    key = held_key.reshape(length, width)
    value = held_value.reshape(length, width)
    upstream = grad_out.reshape(length * group, width)
    tall, short = upstream.shape, key.shape
    grad_q, grad_k, grad_v = pl.pallas_call(
        functools.partial(kernel, sections, parts, tokens, group),
        out_shape=(
            jax.ShapeDtypeStruct(tall, jnp.bfloat16),
            jax.ShapeDtypeStruct(short, jnp.bfloat16),
            jax.ShapeDtypeStruct(short, jnp.bfloat16),
        ),
        in_specs=[pl.BlockSpec(memory_space=pl.ANY)] * 4,
        out_specs=[pl.BlockSpec(memory_space=pltpu.VMEM)] * 3,
        scratch_shapes=[
            pltpu.VMEM(tall, jnp.bfloat16),
            pltpu.VMEM(short, jnp.bfloat16),
            pltpu.VMEM(short, jnp.bfloat16),
            pltpu.VMEM(tall, jnp.bfloat16),
            pltpu.VMEM((width, length), jnp.bfloat16),
            pltpu.VMEM(short, jnp.float32),
            pltpu.VMEM(short, jnp.float32),
            pltpu.SemaphoreType.DMA((parts,)),
            pltpu.SemaphoreType.DMA((parts,)),
        ]
        + [pltpu.SemaphoreType.DMA] * 6,
        compiler_params=pltpu.CompilerParams(
            collective_id=0, has_side_effects=True, vmem_limit_bytes=48 * 1024 * 1024
        ),
    )(query, key, value, upstream)
    return (
        grad_q.reshape(grad_out.shape),
        grad_k.reshape(held_key.shape),
        grad_v.reshape(held_value.shape),
    )


def solution(mesh):
    placed = (
        P("section", "tp", None, None),
        P("section", None, "tp", None),
        P("section", None, "tp", None),
        P("section", None, "tp", None),
    )
    return jax.shard_map(
        local,
        mesh=mesh,
        in_specs=placed,
        out_specs=(
            P("section", None, "tp", None),
            P("section", None, "tp", None),
            P("section", None, "tp", None),
        ),
        check_vma=False,
    )
```

```python
import functools

import jax
import jax.numpy as jnp
from jax import lax
from jax.experimental import pallas as pl
from jax.experimental.pallas import tpu as pltpu
from jax.sharding import PartitionSpec as P

MESH = pl.DeviceIdType.MESH
LOG2E = 1.4426950408889634
SIZE_Z = 4
LATEST = 2
ORDER = (0, 1, 3, 2)
FIRST = (16, 8, 0, 4)
CONTRACT_LAST = (((1,), (1,)), ((), ()))


def local_wait(ref, sem):
    pltpu.make_async_copy(ref, ref, sem).wait()


def kernel(
    sections, parts, tokens, group,
    q_ref, k_ref, v_ref, g_ref,
    dq_ref, dk_ref, dv_ref,
    q_in, k_in, v_in, g_in, q_mid, k_turned, dk_sum, dv_sum,
    q_sem, g_sem, k_sem, v_sem, q_mid_sem, q_out_sem, g_out_sem, k_out_sem, v_out_sem, q_on_sem, all_in,
):
    s = lax.axis_index("section")
    t = lax.axis_index("tp")
    rows = tokens * group
    length = parts * tokens
    width = q_ref.shape[-1]
    scale = width ** (-0.5)
    size_y = parts // SIZE_Z
    y, z = t // SIZE_Z, lax.rem(t, SIZE_Z)
    works = s < sections - 1
    gives = s > 0
    partner = sections - 2 - s
    alone = partner == s
    level = jnp.logical_and(works, lax.rem(s, 4) == 3)
    leads = z == LATEST

    def at(z, y):
        return y * SIZE_Z + z

    def block(index):
        return pl.ds(pl.multiple_of(index * rows, rows), rows)

    def no(condition):
        return jnp.logical_not(condition)

    def both(one, other):
        return jnp.logical_and(one, other)

    barrier = pltpu.get_barrier_semaphore()

    def greet(condition, section, part):
        @pl.when(condition)
        def _():
            pl.semaphore_signal(barrier, inc=1, device_id=(section, part), device_id_type=MESH)

    for other in range(size_y):
        greet(both(works, no(both(alone, y == other))), partner, at(z, other))
        greet(both(works, no(leads)), partner, at(LATEST, other))
    greet(no(leads), s, at(LATEST, y))
    greet(works, s + 1, t)
    own = jnp.where(works, size_y, 0) - jnp.where(alone, 1, 0) + jnp.where(gives, 1, 0)
    others = jnp.where(works, parts - size_y, 0) + SIZE_Z - 1
    pl.semaphore_wait(barrier, own + jnp.where(leads, others, 0))

    @pl.when(leads)
    def _():
        for other in range(SIZE_Z):
            if other != LATEST:
                pl.semaphore_signal(all_in, inc=1, device_id=(s, at(other, y)), device_id_type=MESH)

    def push(condition, origin, target, out_sem, in_sem, section, part):
        @pl.when(condition)
        def _():
            pltpu.make_async_remote_copy(
                src_ref=origin, dst_ref=target, send_sem=out_sem, recv_sem=in_sem,
                device_id=(section, part), device_id_type=MESH,
            ).start()

    def hand_over(origin, target, out_sem, in_sem):
        push(both(works, no(alone)), origin, target, out_sem, in_sem, partner, t)

        @pl.when(alone)
        def _():
            pltpu.make_async_copy(origin, target, in_sem).start()

    def taken(step, section):
        upper = lax.rem(section, 2 * SIZE_Z) >= SIZE_Z
        same = lax.rem(section, 4) == 3
        turned = step // size_y
        apart = jnp.where(
            turned == 0,
            jnp.where(same, 0, jnp.where(upper, 1, 3)),
            jnp.where(
                turned == 1,
                jnp.where(same, 1, 2),
                jnp.where(
                    turned == 2,
                    jnp.where(same, 3, 0),
                    jnp.where(same, 2, jnp.where(upper, 3, 1)),
                ),
            ),
        )
        return at(lax.rem(z + apart, SIZE_Z), lax.rem(y + size_y - lax.rem(step, size_y), size_y))

    def send_upstream(step, carry):
        index = taken(step, s - 1)
        push(gives, g_ref.at[block(index)], g_in.at[block(index)], g_out_sem, g_sem.at[index], s - 1, t)
        return carry

    def send_query(to):
        itself = both(alone, to == t)
        push(
            both(works, no(itself)),
            q_ref.at[block(to)], q_in.at[block(t)], q_out_sem, q_sem.at[t], partner, to,
        )

        @pl.when(both(works, itself))
        def _():
            pltpu.make_async_copy(q_ref.at[block(to)], q_in.at[block(t)], q_sem.at[t]).start()

    def detour(to_z, to_y):
        return both(level, both(lax.rem(to_z + SIZE_Z - z, SIZE_Z) == 2, lax.rem(y + to_y, 2) == 0))

    def send_beside(step, carry):
        send_query(at(z, lax.rem(y + step, size_y)))
        return carry

    def send_round(step, carry):
        to_y = lax.rem(y + 2 * step, size_y)
        to_z = lax.rem(z + 2, SIZE_Z)
        slot = y // 2
        push(
            level, q_ref.at[block(at(to_z, to_y))], q_mid.at[block(slot)], q_out_sem, q_mid_sem.at[slot],
            partner, at(lax.rem(z + 1, SIZE_Z), to_y),
        )
        return carry

    def send_across(step, carry):
        turn = step // size_y
        to_z = jnp.where(turn == 0, ORDER[0], jnp.where(turn == 1, ORDER[1], jnp.where(turn == 2, ORDER[2], ORDER[3])))
        to_y = lax.rem(y + step, size_y)

        @pl.when(both(to_z != z, no(detour(to_z, to_y))))
        def _():
            send_query(at(to_z, to_y))

        return carry

    def send_pair():
        hand_over(k_ref, k_in, k_out_sem, k_sem)
        hand_over(v_ref, v_in, v_out_sem, v_sem)

    first = jnp.where(z == 0, FIRST[0], jnp.where(z == 1, FIRST[1], jnp.where(z == 2, FIRST[2], FIRST[3])))

    @pl.when(no(leads))
    def _():
        send_pair()
        lax.fori_loop(0, first, send_upstream, 0)
        lax.fori_loop(0, size_y, send_beside, 0)
        pl.semaphore_wait(all_in, 1)

    lax.fori_loop(0, 2, send_round, 0)
    lax.fori_loop(0, size_y, send_across, 0)

    @pl.when(leads)
    def _():
        send_pair()

    lax.fori_loop(size_y, 2 * size_y, send_across, 0)

    @pl.when(leads)
    def _():
        lax.fori_loop(0, size_y, send_beside, 0)

    lax.fori_loop(2 * size_y, parts, send_across, 0)

    lax.fori_loop(jnp.where(leads, 0, first), parts, send_upstream, 0)

    @pl.when(level)
    def _():
        def on(slot, carry):
            from_y = 2 * slot + lax.rem(y, 2)
            sender = at(lax.rem(z + SIZE_Z - 1, SIZE_Z), from_y)
            local_wait(q_mid.at[block(slot)], q_mid_sem.at[slot])
            push(
                level, q_mid.at[block(slot)], q_in.at[block(sender)], q_on_sem, q_sem.at[sender],
                s, at(lax.rem(z + 1, SIZE_Z), y),
            )
            return carry

        lax.fori_loop(0, 2, on, 0)

    dk_sum[...] = jnp.zeros_like(dk_sum)
    dv_sum[...] = jnp.zeros_like(dv_sum)

    def backward(index, keys):
        here = block(index)
        query, upstream = q_in[here, :], g_in[here, :]
        span = length // 4
        pieces = keys // span
        token = index * tokens - (keys - span) + lax.broadcasted_iota(jnp.int32, (span, rows), 1) // group
        seen = lax.broadcasted_iota(jnp.int32, (span, rows), 0) <= token
        scores = []
        for piece in range(pieces):
            part = lax.dot_general(
                k_in[piece * span : (piece + 1) * span, :], query, CONTRACT_LAST, preferred_element_type=jnp.float32
            )
            scores.append(jnp.where(seen, part, -1e30) if piece == pieces - 1 else part)
        top = functools.reduce(jnp.maximum, [jnp.max(part, axis=0, keepdims=True) for part in scores])
        base = top * (scale * LOG2E)
        weights = [jnp.exp2(part * (scale * LOG2E) - base) for part in scores]
        share = 1.0 / sum(jnp.sum(part, axis=0, keepdims=True) for part in weights)
        grads = [
            lax.dot_general(
                v_in[piece * span : (piece + 1) * span, :], upstream, CONTRACT_LAST, preferred_element_type=jnp.float32
            )
            for piece in range(pieces)
        ]
        probs = [part * share for part in weights]
        delta = sum(jnp.sum(p * g, axis=0, keepdims=True) for p, g in zip(probs, grads))
        turned = None
        for piece in range(pieces):
            at_keys = slice(piece * span, (piece + 1) * span)
            dv_sum[at_keys, :] += jnp.dot(
                probs[piece].astype(jnp.bfloat16), upstream, preferred_element_type=jnp.float32
            )
            grad_scores = (probs[piece] * (grads[piece] - delta)).astype(jnp.bfloat16)
            dk_sum[at_keys, :] += jnp.dot(grad_scores, query, preferred_element_type=jnp.float32)
            part = jnp.dot(k_turned[:, at_keys], grad_scores, preferred_element_type=jnp.float32)
            turned = part if turned is None else turned + part
        dq_ref[here, :] = (turned * scale).T.astype(dq_ref.dtype)

    @pl.when(works)
    def _():
        local_wait(k_in, k_sem)
        local_wait(v_in, v_sem)
        k_turned[...] = k_in[...].T

        def take(step, carry):
            index = taken(step, s)
            local_wait(q_in.at[block(index)], q_sem.at[index])
            local_wait(g_in.at[block(index)], g_sem.at[index])
            spans = 4
            for span in range(spans):
                @pl.when(index // (parts // spans) == span)
                def _():
                    backward(index, (span + 1) * length // spans)
            return carry

        lax.fori_loop(0, parts, take, 0)

    @pl.when(no(works))
    def _():
        dq_ref[...] = jnp.zeros_like(dq_ref)

    dk_ref[...] = (dk_sum[...] * scale).astype(dk_ref.dtype)
    dv_ref[...] = dv_sum[...].astype(dv_ref.dtype)

    @pl.when(both(works, no(alone)))
    def _():
        local_wait(k_ref, k_out_sem)
        local_wait(v_ref, v_out_sem)
        local_wait(q_ref, q_out_sem)

    @pl.when(alone)
    def _():
        local_wait(q_ref.at[pl.ds(0, (parts - 1) * rows)], q_out_sem)

    @pl.when(level)
    def _():
        local_wait(q_mid, q_on_sem)

    @pl.when(gives)
    def _():
        local_wait(g_ref, g_out_sem)


def local(held_query, held_key, held_value, grad_out):
    sections, parts = lax.axis_size("section"), lax.axis_size("tp")
    _, tokens, heads, width = held_query.shape
    length = held_key.shape[1]
    group = heads // parts
    query = held_query.reshape(tokens, parts, group, width)
    query = jnp.swapaxes(query, 0, 1).reshape(parts * tokens * group, width)
    key = held_key.reshape(length, width)
    value = held_value.reshape(length, width)
    upstream = grad_out.reshape(length * group, width)
    tall, short = upstream.shape, key.shape
    grad_q, grad_k, grad_v = pl.pallas_call(
        functools.partial(kernel, sections, parts, tokens, group),
        out_shape=(
            jax.ShapeDtypeStruct(tall, jnp.bfloat16),
            jax.ShapeDtypeStruct(short, jnp.bfloat16),
            jax.ShapeDtypeStruct(short, jnp.bfloat16),
        ),
        in_specs=[pl.BlockSpec(memory_space=pl.ANY)] * 4,
        out_specs=[pl.BlockSpec(memory_space=pltpu.VMEM)] * 3,
        scratch_shapes=[
            pltpu.VMEM(tall, jnp.bfloat16),
            pltpu.VMEM(short, jnp.bfloat16),
            pltpu.VMEM(short, jnp.bfloat16),
            pltpu.VMEM(tall, jnp.bfloat16),
            pltpu.VMEM((2 * tokens * group, width), jnp.bfloat16),
            pltpu.VMEM((width, length), jnp.bfloat16),
            pltpu.VMEM(short, jnp.float32),
            pltpu.VMEM(short, jnp.float32),
            pltpu.SemaphoreType.DMA((parts,)),
            pltpu.SemaphoreType.DMA((parts,)),
        ]
        + [pltpu.SemaphoreType.DMA] * 2
        + [pltpu.SemaphoreType.DMA((2,))]
        + [pltpu.SemaphoreType.DMA] * 5
        + [pltpu.SemaphoreType.REGULAR],
        compiler_params=pltpu.CompilerParams(
            collective_id=0, has_side_effects=True, vmem_limit_bytes=48 * 1024 * 1024
        ),
    )(query, key, value, upstream)
    return (
        grad_q.reshape(grad_out.shape),
        grad_k.reshape(held_key.shape),
        grad_v.reshape(held_value.shape),
    )


def solution(mesh):
    placed = (
        P("section", "tp", None, None),
        P("section", None, "tp", None),
        P("section", None, "tp", None),
        P("section", None, "tp", None),
    )
    return jax.shard_map(
        local,
        mesh=mesh,
        in_specs=placed,
        out_specs=(
            P("section", None, "tp", None),
            P("section", None, "tp", None),
            P("section", None, "tp", None),
        ),
        check_vma=False,
    )
```

```python
import functools

import jax
import jax.numpy as jnp
from jax import lax
from jax.experimental import pallas as pl
from jax.experimental.pallas import tpu as pltpu
from jax.sharding import PartitionSpec as P

MESH = pl.DeviceIdType.MESH
LOG2E = 1.4426950408889634
SIZE_Z = 4
LATEST = 2
ORDER = (0, 1, 3, 2)
FIRST = (16, 4, 0, 0)
CONTRACT_LAST = (((1,), (1,)), ((), ()))


def local_wait(ref, sem):
    pltpu.make_async_copy(ref, ref, sem).wait()


def kernel(
    sections, parts, tokens, group,
    q_ref, k_ref, v_ref, g_ref,
    dq_ref, dk_ref, dv_ref,
    q_in, k_in, v_in, g_in, q_mid, k_turned, dk_sum, dv_sum,
    q_sem, g_sem, k_sem, v_sem, q_mid_sem, q_out_sem, g_out_sem, k_out_sem, v_out_sem, q_on_sem, all_in,
):
    s = lax.axis_index("section")
    t = lax.axis_index("tp")
    rows = tokens * group
    length = parts * tokens
    width = q_ref.shape[-1]
    scale = width ** (-0.5)
    size_y = parts // SIZE_Z
    y, z = t // SIZE_Z, lax.rem(t, SIZE_Z)
    works = s < sections - 1
    gives = s > 0
    partner = sections - 2 - s
    alone = partner == s
    level = jnp.logical_and(works, lax.rem(s, 4) == 3)
    leads = z == LATEST

    def at(z, y):
        return y * SIZE_Z + z

    def block(index):
        return pl.ds(pl.multiple_of(index * rows, rows), rows)

    def no(condition):
        return jnp.logical_not(condition)

    def both(one, other):
        return jnp.logical_and(one, other)

    barrier = pltpu.get_barrier_semaphore()

    def greet(condition, section, part):
        @pl.when(condition)
        def _():
            pl.semaphore_signal(barrier, inc=1, device_id=(section, part), device_id_type=MESH)

    for other in range(size_y):
        greet(both(works, no(both(alone, y == other))), partner, at(z, other))
        greet(both(works, no(leads)), partner, at(LATEST, other))
    greet(no(leads), s, at(LATEST, y))
    greet(works, s + 1, t)
    own = jnp.where(works, size_y, 0) - jnp.where(alone, 1, 0) + jnp.where(gives, 1, 0)
    others = jnp.where(works, parts - size_y, 0) + SIZE_Z - 1
    pl.semaphore_wait(barrier, own + jnp.where(leads, others, 0))

    @pl.when(leads)
    def _():
        for other in range(SIZE_Z):
            if other != LATEST:
                pl.semaphore_signal(all_in, inc=1, device_id=(s, at(other, y)), device_id_type=MESH)

    def push(condition, origin, target, out_sem, in_sem, section, part):
        @pl.when(condition)
        def _():
            pltpu.make_async_remote_copy(
                src_ref=origin, dst_ref=target, send_sem=out_sem, recv_sem=in_sem,
                device_id=(section, part), device_id_type=MESH,
            ).start()

    def hand_over(origin, target, out_sem, in_sem):
        push(both(works, no(alone)), origin, target, out_sem, in_sem, partner, t)

        @pl.when(alone)
        def _():
            pltpu.make_async_copy(origin, target, in_sem).start()

    def taken(step, section):
        upper = lax.rem(section, 2 * SIZE_Z) >= SIZE_Z
        same = lax.rem(section, 4) == 3
        turned = step // size_y
        apart = jnp.where(
            turned == 0,
            jnp.where(same, 0, jnp.where(upper, 1, 3)),
            jnp.where(
                turned == 1,
                jnp.where(same, 1, 2),
                jnp.where(
                    turned == 2,
                    jnp.where(same, 3, 0),
                    jnp.where(same, 2, jnp.where(upper, 3, 1)),
                ),
            ),
        )
        return at(lax.rem(z + apart, SIZE_Z), lax.rem(y + size_y - lax.rem(step, size_y), size_y))

    def send_upstream(step, carry):
        index = taken(step, s - 1)
        push(gives, g_ref.at[block(index)], g_in.at[block(index)], g_out_sem, g_sem.at[index], s - 1, t)
        return carry

    def send_query(to):
        itself = both(alone, to == t)
        push(
            both(works, no(itself)),
            q_ref.at[block(to)], q_in.at[block(t)], q_out_sem, q_sem.at[t], partner, to,
        )

        @pl.when(both(works, itself))
        def _():
            pltpu.make_async_copy(q_ref.at[block(to)], q_in.at[block(t)], q_sem.at[t]).start()

    def detour(to_z, to_y):
        return both(level, both(lax.rem(to_z + SIZE_Z - z, SIZE_Z) == 2, lax.rem(y + to_y, 2) == 0))

    def send_beside(step, carry):
        send_query(at(z, lax.rem(y + step, size_y)))
        return carry

    def send_round(step, carry):
        to_y = lax.rem(y + 2 * step, size_y)
        to_z = lax.rem(z + 2, SIZE_Z)
        slot = y // 2
        push(
            level, q_ref.at[block(at(to_z, to_y))], q_mid.at[block(slot)], q_out_sem, q_mid_sem.at[slot],
            partner, at(lax.rem(z + 1, SIZE_Z), to_y),
        )
        return carry

    def send_across(step, carry):
        turn = step // size_y
        to_z = jnp.where(turn == 0, ORDER[0], jnp.where(turn == 1, ORDER[1], jnp.where(turn == 2, ORDER[2], ORDER[3])))
        to_y = lax.rem(y + step, size_y)

        @pl.when(both(to_z != z, no(detour(to_z, to_y))))
        def _():
            send_query(at(to_z, to_y))

        return carry

    def send_pair():
        hand_over(k_ref, k_in, k_out_sem, k_sem)
        hand_over(v_ref, v_in, v_out_sem, v_sem)

    first = jnp.where(z == 0, FIRST[0], jnp.where(z == 1, FIRST[1], jnp.where(z == 2, FIRST[2], FIRST[3])))

    @pl.when(no(leads))
    def _():
        send_pair()
        lax.fori_loop(0, first, send_upstream, 0)
        @pl.when(z == 0)
        def _():
            lax.fori_loop(0, size_y, send_beside, 0)

        pl.semaphore_wait(all_in, 1)

    lax.fori_loop(0, 2, send_round, 0)
    lax.fori_loop(0, size_y, send_across, 0)

    @pl.when(leads)
    def _():
        send_pair()

    @pl.when(both(z != 0, no(leads)))
    def _():
        lax.fori_loop(0, size_y, send_beside, 0)

    lax.fori_loop(size_y, 2 * size_y, send_across, 0)

    @pl.when(leads)
    def _():
        lax.fori_loop(0, size_y, send_beside, 0)

    lax.fori_loop(2 * size_y, parts, send_across, 0)

    lax.fori_loop(jnp.where(leads, 0, first), parts, send_upstream, 0)

    @pl.when(level)
    def _():
        def on(slot, carry):
            from_y = 2 * slot + lax.rem(y, 2)
            sender = at(lax.rem(z + SIZE_Z - 1, SIZE_Z), from_y)
            local_wait(q_mid.at[block(slot)], q_mid_sem.at[slot])
            push(
                level, q_mid.at[block(slot)], q_in.at[block(sender)], q_on_sem, q_sem.at[sender],
                s, at(lax.rem(z + 1, SIZE_Z), y),
            )
            return carry

        lax.fori_loop(0, 2, on, 0)

    dk_sum[...] = jnp.zeros_like(dk_sum)
    dv_sum[...] = jnp.zeros_like(dv_sum)

    def backward(index, keys):
        here = block(index)
        query, upstream = q_in[here, :], g_in[here, :]
        span = length // 4
        pieces = keys // span
        token = index * tokens - (keys - span) + lax.broadcasted_iota(jnp.int32, (span, rows), 1) // group
        seen = lax.broadcasted_iota(jnp.int32, (span, rows), 0) <= token
        scores = []
        for piece in range(pieces):
            part = lax.dot_general(
                k_in[piece * span : (piece + 1) * span, :], query, CONTRACT_LAST, preferred_element_type=jnp.float32
            )
            scores.append(jnp.where(seen, part, -1e30) if piece == pieces - 1 else part)
        top = functools.reduce(jnp.maximum, [jnp.max(part, axis=0, keepdims=True) for part in scores])
        base = top * (scale * LOG2E)
        weights = [jnp.exp2(part * (scale * LOG2E) - base) for part in scores]
        share = 1.0 / sum(jnp.sum(part, axis=0, keepdims=True) for part in weights)
        grads = [
            lax.dot_general(
                v_in[piece * span : (piece + 1) * span, :], upstream, CONTRACT_LAST, preferred_element_type=jnp.float32
            )
            for piece in range(pieces)
        ]
        probs = [part * share for part in weights]
        delta = sum(jnp.sum(p * g, axis=0, keepdims=True) for p, g in zip(probs, grads))
        turned = None
        for piece in range(pieces):
            at_keys = slice(piece * span, (piece + 1) * span)
            dv_sum[at_keys, :] += jnp.dot(
                probs[piece].astype(jnp.bfloat16), upstream, preferred_element_type=jnp.float32
            )
            grad_scores = (probs[piece] * (grads[piece] - delta) * scale).astype(jnp.bfloat16)
            dk_sum[at_keys, :] += jnp.dot(grad_scores, query, preferred_element_type=jnp.float32)
            part = jnp.dot(k_turned[:, at_keys], grad_scores, preferred_element_type=jnp.float32)
            turned = part if turned is None else turned + part
        dq_ref[here, :] = turned.T.astype(dq_ref.dtype)

    @pl.when(works)
    def _():
        local_wait(k_in, k_sem)
        local_wait(v_in, v_sem)
        k_turned[...] = k_in[...].T

        def take(step, carry):
            index = taken(step, s)
            local_wait(q_in.at[block(index)], q_sem.at[index])
            local_wait(g_in.at[block(index)], g_sem.at[index])
            spans = 4
            for span in range(spans):
                @pl.when(index // (parts // spans) == span)
                def _():
                    backward(index, (span + 1) * length // spans)
            return carry

        lax.fori_loop(0, parts, take, 0)

    @pl.when(no(works))
    def _():
        dq_ref[...] = jnp.zeros_like(dq_ref)

    dk_ref[...] = dk_sum[...].astype(dk_ref.dtype)
    dv_ref[...] = dv_sum[...].astype(dv_ref.dtype)

    @pl.when(both(works, no(alone)))
    def _():
        local_wait(k_ref, k_out_sem)
        local_wait(v_ref, v_out_sem)
        local_wait(q_ref, q_out_sem)

    @pl.when(alone)
    def _():
        local_wait(q_ref.at[pl.ds(0, (parts - 1) * rows)], q_out_sem)

    @pl.when(level)
    def _():
        local_wait(q_mid, q_on_sem)

    @pl.when(gives)
    def _():
        local_wait(g_ref, g_out_sem)


def write_out(q_ref, k_ref, v_ref, dq_ref, dk_ref, dv_ref, q_sem, k_sem, v_sem):
    copies = [
        pltpu.make_async_copy(q_ref, dq_ref, q_sem),
        pltpu.make_async_copy(k_ref, dk_ref, k_sem),
        pltpu.make_async_copy(v_ref, dv_ref, v_sem),
    ]
    for copy in copies:
        copy.start()
    for copy in copies:
        copy.wait()


def local(held_query, held_key, held_value, grad_out):
    sections, parts = lax.axis_size("section"), lax.axis_size("tp")
    _, tokens, heads, width = held_query.shape
    length = held_key.shape[1]
    group = heads // parts
    query = held_query.reshape(tokens, parts, group, width)
    query = jnp.swapaxes(query, 0, 1).reshape(parts * tokens * group, width)
    key = held_key.reshape(length, width)
    value = held_value.reshape(length, width)
    upstream = grad_out.reshape(length * group, width)
    tall, short = upstream.shape, key.shape
    grad_q, grad_k, grad_v = pl.pallas_call(
        functools.partial(kernel, sections, parts, tokens, group),
        out_shape=(
            jax.ShapeDtypeStruct(tall, jnp.bfloat16),
            jax.ShapeDtypeStruct(short, jnp.bfloat16),
            jax.ShapeDtypeStruct(short, jnp.bfloat16),
        ),
        in_specs=[pl.BlockSpec(memory_space=pl.ANY)] * 4,
        out_specs=[pl.BlockSpec(memory_space=pltpu.VMEM)] * 3,
        scratch_shapes=[
            pltpu.VMEM(tall, jnp.bfloat16),
            pltpu.VMEM(short, jnp.bfloat16),
            pltpu.VMEM(short, jnp.bfloat16),
            pltpu.VMEM(tall, jnp.bfloat16),
            pltpu.VMEM((2 * tokens * group, width), jnp.bfloat16),
            pltpu.VMEM((width, length), jnp.bfloat16),
            pltpu.VMEM(short, jnp.float32),
            pltpu.VMEM(short, jnp.float32),
            pltpu.SemaphoreType.DMA((parts,)),
            pltpu.SemaphoreType.DMA((parts,)),
        ]
        + [pltpu.SemaphoreType.DMA] * 2
        + [pltpu.SemaphoreType.DMA((2,))]
        + [pltpu.SemaphoreType.DMA] * 5
        + [pltpu.SemaphoreType.REGULAR],
        compiler_params=pltpu.CompilerParams(
            collective_id=0, has_side_effects=True, vmem_limit_bytes=48 * 1024 * 1024
        ),
    )(query, key, value, upstream)
    grad_q, grad_k, grad_v = pl.pallas_call(
        write_out,
        out_shape=(
            jax.ShapeDtypeStruct(tall, jnp.bfloat16),
            jax.ShapeDtypeStruct(short, jnp.bfloat16),
            jax.ShapeDtypeStruct(short, jnp.bfloat16),
        ),
        in_specs=[pl.BlockSpec(memory_space=pl.ANY)] * 3,
        out_specs=[pl.BlockSpec(memory_space=pl.ANY)] * 3,
        scratch_shapes=[pltpu.SemaphoreType.DMA] * 3,
        compiler_params=pltpu.CompilerParams(vmem_limit_bytes=48 * 1024 * 1024),
    )(grad_q, grad_k, grad_v)
    return (
        grad_q.reshape(grad_out.shape),
        grad_k.reshape(held_key.shape),
        grad_v.reshape(held_value.shape),
    )


def solution(mesh):
    placed = (
        P("section", "tp", None, None),
        P("section", None, "tp", None),
        P("section", None, "tp", None),
        P("section", None, "tp", None),
    )
    return jax.shard_map(
        local,
        mesh=mesh,
        in_specs=placed,
        out_specs=(
            P("section", None, "tp", None),
            P("section", None, "tp", None),
            P("section", None, "tp", None),
        ),
        check_vma=False,
    )
```

```python
import functools

import jax
import jax.numpy as jnp
from jax import lax
from jax.experimental import pallas as pl
from jax.experimental.pallas import tpu as pltpu
from jax.sharding import PartitionSpec as P

MESH = pl.DeviceIdType.MESH
LOG2E = 1.4426950408889634
SIZE_Z = 4
LATEST = 2
ORDER = (0, 1, 3, 2)
FIRST = (16, 4, 0, 0)
CONTRACT_LAST = (((1,), (1,)), ((), ()))


def local_wait(ref, sem):
    pltpu.make_async_copy(ref, ref, sem).wait()


def kernel(
    sections, parts, tokens, group,
    q_ref, k_ref, v_ref, g_ref,
    dq_ref, dk_ref, dv_ref,
    q_in, k_in, v_in, g_in, q_mid, k_turned, dk_sum, dv_sum,
    q_sem, g_sem, k_sem, v_sem, q_mid_sem, q_out_sem, g_out_sem, k_out_sem, v_out_sem, q_on_sem, all_in,
):
    s = lax.axis_index("section")
    t = lax.axis_index("tp")
    rows = tokens * group
    length = parts * tokens
    width = q_ref.shape[-1]
    scale = width ** (-0.5)
    size_y = parts // SIZE_Z
    y, z = t // SIZE_Z, lax.rem(t, SIZE_Z)
    works = s < sections - 1
    gives = s > 0
    partner = sections - 2 - s
    alone = partner == s
    level = jnp.logical_and(works, lax.rem(s, 4) == 3)
    leads = z == LATEST

    def at(z, y):
        return y * SIZE_Z + z

    def block(index):
        return pl.ds(pl.multiple_of(index * rows, rows), rows)

    def no(condition):
        return jnp.logical_not(condition)

    def both(one, other):
        return jnp.logical_and(one, other)

    barrier = pltpu.get_barrier_semaphore()

    def greet(condition, section, part):
        @pl.when(condition)
        def _():
            pl.semaphore_signal(barrier, inc=1, device_id=(section, part), device_id_type=MESH)

    for other in range(size_y):
        greet(both(works, no(both(alone, y == other))), partner, at(z, other))
        greet(both(works, no(leads)), partner, at(LATEST, other))
    greet(no(leads), s, at(LATEST, y))
    greet(works, s + 1, t)
    own = jnp.where(works, size_y, 0) - jnp.where(alone, 1, 0) + jnp.where(gives, 1, 0)
    others = jnp.where(works, parts - size_y, 0) + SIZE_Z - 1
    pl.semaphore_wait(barrier, own + jnp.where(leads, others, 0))

    @pl.when(leads)
    def _():
        for other in range(SIZE_Z):
            if other != LATEST:
                pl.semaphore_signal(all_in, inc=1, device_id=(s, at(other, y)), device_id_type=MESH)

    def push(condition, origin, target, out_sem, in_sem, section, part):
        @pl.when(condition)
        def _():
            pltpu.make_async_remote_copy(
                src_ref=origin, dst_ref=target, send_sem=out_sem, recv_sem=in_sem,
                device_id=(section, part), device_id_type=MESH,
            ).start()

    def hand_over(origin, target, out_sem, in_sem):
        push(both(works, no(alone)), origin, target, out_sem, in_sem, partner, t)

        @pl.when(alone)
        def _():
            pltpu.make_async_copy(origin, target, in_sem).start()

    def taken(step, section):
        upper = lax.rem(section, 2 * SIZE_Z) >= SIZE_Z
        same = lax.rem(section, 4) == 3
        turned = step // size_y
        apart = jnp.where(
            turned == 0,
            jnp.where(same, 0, jnp.where(upper, 1, 3)),
            jnp.where(
                turned == 1,
                jnp.where(same, 1, 2),
                jnp.where(
                    turned == 2,
                    jnp.where(same, 3, 0),
                    jnp.where(same, 2, jnp.where(upper, 3, 1)),
                ),
            ),
        )
        return at(lax.rem(z + apart, SIZE_Z), lax.rem(y + size_y - lax.rem(step, size_y), size_y))

    def send_upstream(step, carry):
        index = taken(step, s - 1)
        push(gives, g_ref.at[block(index)], g_in.at[block(index)], g_out_sem, g_sem.at[index], s - 1, t)
        return carry

    def send_query(to):
        itself = both(alone, to == t)
        push(
            both(works, no(itself)),
            q_ref.at[block(to)], q_in.at[block(t)], q_out_sem, q_sem.at[t], partner, to,
        )

        @pl.when(both(works, itself))
        def _():
            pltpu.make_async_copy(q_ref.at[block(to)], q_in.at[block(t)], q_sem.at[t]).start()

    def detour(to_z, to_y):
        return both(level, both(lax.rem(to_z + SIZE_Z - z, SIZE_Z) == 2, lax.rem(y + to_y, 2) == 0))

    def send_beside(step, carry):
        send_query(at(z, lax.rem(y + step, size_y)))
        return carry

    def send_round(step, carry):
        to_y = lax.rem(y + 2 * step, size_y)
        to_z = lax.rem(z + 2, SIZE_Z)
        slot = y // 2
        push(
            level, q_ref.at[block(at(to_z, to_y))], q_mid.at[block(slot)], q_out_sem, q_mid_sem.at[slot],
            partner, at(lax.rem(z + 1, SIZE_Z), to_y),
        )
        return carry

    def send_across(step, carry):
        turn = step // size_y
        to_z = jnp.where(turn == 0, ORDER[0], jnp.where(turn == 1, ORDER[1], jnp.where(turn == 2, ORDER[2], ORDER[3])))
        to_y = lax.rem(y + step, size_y)

        @pl.when(both(to_z != z, no(detour(to_z, to_y))))
        def _():
            send_query(at(to_z, to_y))

        return carry

    def send_pair():
        hand_over(k_ref, k_in, k_out_sem, k_sem)
        hand_over(v_ref, v_in, v_out_sem, v_sem)

    first = jnp.where(z == 0, FIRST[0], jnp.where(z == 1, FIRST[1], jnp.where(z == 2, FIRST[2], FIRST[3])))

    @pl.when(no(leads))
    def _():
        send_pair()
        lax.fori_loop(0, first, send_upstream, 0)
        @pl.when(z == 0)
        def _():
            lax.fori_loop(0, size_y, send_beside, 0)

        pl.semaphore_wait(all_in, 1)

    lax.fori_loop(0, 2, send_round, 0)
    lax.fori_loop(0, size_y, send_across, 0)

    @pl.when(leads)
    def _():
        send_pair()

    @pl.when(both(z != 0, no(leads)))
    def _():
        lax.fori_loop(0, size_y, send_beside, 0)

    lax.fori_loop(size_y, 2 * size_y, send_across, 0)

    @pl.when(leads)
    def _():
        lax.fori_loop(0, size_y, send_beside, 0)

    lax.fori_loop(2 * size_y, parts, send_across, 0)

    lax.fori_loop(jnp.where(leads, 0, first), parts, send_upstream, 0)

    @pl.when(level)
    def _():
        def on(slot, carry):
            from_y = 2 * slot + lax.rem(y, 2)
            sender = at(lax.rem(z + SIZE_Z - 1, SIZE_Z), from_y)
            local_wait(q_mid.at[block(slot)], q_mid_sem.at[slot])
            push(
                level, q_mid.at[block(slot)], q_in.at[block(sender)], q_on_sem, q_sem.at[sender],
                s, at(lax.rem(z + 1, SIZE_Z), y),
            )
            return carry

        lax.fori_loop(0, 2, on, 0)

    dk_sum[...] = jnp.zeros_like(dk_sum)
    dv_sum[...] = jnp.zeros_like(dv_sum)

    def backward(index, keys):
        here = block(index)
        query, upstream = q_in[here, :], g_in[here, :]
        wide = length // 4
        starts = list(range(0, keys, wide))
        spans = [slice(start, min(start + wide, keys)) for start in starts]
        pieces = len(spans)
        edge = keys - starts[-1]
        token = index * tokens - starts[-1] + lax.broadcasted_iota(jnp.int32, (edge, rows), 1) // group
        seen = lax.broadcasted_iota(jnp.int32, (edge, rows), 0) <= token
        scores = []
        for piece in range(pieces):
            part = lax.dot_general(
                k_in[spans[piece], :], query, CONTRACT_LAST, preferred_element_type=jnp.float32
            )
            scores.append(jnp.where(seen, part, -1e30) if piece == pieces - 1 else part)
        top = functools.reduce(jnp.maximum, [jnp.max(part, axis=0, keepdims=True) for part in scores])
        base = top * (scale * LOG2E)
        weights = [jnp.exp2(part * (scale * LOG2E) - base) for part in scores]
        share = 1.0 / sum(jnp.sum(part, axis=0, keepdims=True) for part in weights)
        grads = [
            lax.dot_general(
                v_in[spans[piece], :], upstream, CONTRACT_LAST, preferred_element_type=jnp.float32
            )
            for piece in range(pieces)
        ]
        probs = [part * share for part in weights]
        delta = sum(jnp.sum(p * g, axis=0, keepdims=True) for p, g in zip(probs, grads))
        turned = None
        for piece in range(pieces):
            at_keys = spans[piece]
            dv_sum[at_keys, :] += jnp.dot(
                probs[piece].astype(jnp.bfloat16), upstream, preferred_element_type=jnp.float32
            )
            grad_scores = (probs[piece] * (grads[piece] - delta) * scale).astype(jnp.bfloat16)
            dk_sum[at_keys, :] += jnp.dot(grad_scores, query, preferred_element_type=jnp.float32)
            part = jnp.dot(k_turned[:, at_keys], grad_scores, preferred_element_type=jnp.float32)
            turned = part if turned is None else turned + part
        dq_ref[here, :] = turned.T.astype(dq_ref.dtype)

    @pl.when(works)
    def _():
        local_wait(k_in, k_sem)
        local_wait(v_in, v_sem)
        k_turned[...] = k_in[...].T

        def take(step, carry):
            index = taken(step, s)
            local_wait(q_in.at[block(index)], q_sem.at[index])
            local_wait(g_in.at[block(index)], g_sem.at[index])
            spans = 8
            for span in range(spans):
                @pl.when(index // (parts // spans) == span)
                def _():
                    backward(index, (span + 1) * length // spans)
            return carry

        lax.fori_loop(0, parts, take, 0)

    @pl.when(no(works))
    def _():
        dq_ref[...] = jnp.zeros_like(dq_ref)

    dk_ref[...] = dk_sum[...].astype(dk_ref.dtype)
    dv_ref[...] = dv_sum[...].astype(dv_ref.dtype)

    @pl.when(both(works, no(alone)))
    def _():
        local_wait(k_ref, k_out_sem)
        local_wait(v_ref, v_out_sem)
        local_wait(q_ref, q_out_sem)

    @pl.when(alone)
    def _():
        local_wait(q_ref.at[pl.ds(0, (parts - 1) * rows)], q_out_sem)

    @pl.when(level)
    def _():
        local_wait(q_mid, q_on_sem)

    @pl.when(gives)
    def _():
        local_wait(g_ref, g_out_sem)


def write_out(q_ref, k_ref, v_ref, dq_ref, dk_ref, dv_ref, q_sem, k_sem, v_sem):
    copies = [
        pltpu.make_async_copy(q_ref, dq_ref, q_sem),
        pltpu.make_async_copy(k_ref, dk_ref, k_sem),
        pltpu.make_async_copy(v_ref, dv_ref, v_sem),
    ]
    for copy in copies:
        copy.start()
    for copy in copies:
        copy.wait()


def local(held_query, held_key, held_value, grad_out):
    sections, parts = lax.axis_size("section"), lax.axis_size("tp")
    _, tokens, heads, width = held_query.shape
    length = held_key.shape[1]
    group = heads // parts
    query = held_query.reshape(tokens, parts, group, width)
    query = jnp.swapaxes(query, 0, 1).reshape(parts * tokens * group, width)
    key = held_key.reshape(length, width)
    value = held_value.reshape(length, width)
    upstream = grad_out.reshape(length * group, width)
    tall, short = upstream.shape, key.shape
    grad_q, grad_k, grad_v = pl.pallas_call(
        functools.partial(kernel, sections, parts, tokens, group),
        out_shape=(
            jax.ShapeDtypeStruct(tall, jnp.bfloat16),
            jax.ShapeDtypeStruct(short, jnp.bfloat16),
            jax.ShapeDtypeStruct(short, jnp.bfloat16),
        ),
        in_specs=[pl.BlockSpec(memory_space=pl.ANY)] * 4,
        out_specs=[pl.BlockSpec(memory_space=pltpu.VMEM)] * 3,
        scratch_shapes=[
            pltpu.VMEM(tall, jnp.bfloat16),
            pltpu.VMEM(short, jnp.bfloat16),
            pltpu.VMEM(short, jnp.bfloat16),
            pltpu.VMEM(tall, jnp.bfloat16),
            pltpu.VMEM((2 * tokens * group, width), jnp.bfloat16),
            pltpu.VMEM((width, length), jnp.bfloat16),
            pltpu.VMEM(short, jnp.float32),
            pltpu.VMEM(short, jnp.float32),
            pltpu.SemaphoreType.DMA((parts,)),
            pltpu.SemaphoreType.DMA((parts,)),
        ]
        + [pltpu.SemaphoreType.DMA] * 2
        + [pltpu.SemaphoreType.DMA((2,))]
        + [pltpu.SemaphoreType.DMA] * 5
        + [pltpu.SemaphoreType.REGULAR],
        compiler_params=pltpu.CompilerParams(
            collective_id=0, has_side_effects=True, vmem_limit_bytes=48 * 1024 * 1024
        ),
    )(query, key, value, upstream)
    grad_q, grad_k, grad_v = pl.pallas_call(
        write_out,
        out_shape=(
            jax.ShapeDtypeStruct(tall, jnp.bfloat16),
            jax.ShapeDtypeStruct(short, jnp.bfloat16),
            jax.ShapeDtypeStruct(short, jnp.bfloat16),
        ),
        in_specs=[pl.BlockSpec(memory_space=pl.ANY)] * 3,
        out_specs=[pl.BlockSpec(memory_space=pl.ANY)] * 3,
        scratch_shapes=[pltpu.SemaphoreType.DMA] * 3,
        compiler_params=pltpu.CompilerParams(vmem_limit_bytes=48 * 1024 * 1024),
    )(grad_q, grad_k, grad_v)
    return (
        grad_q.reshape(grad_out.shape),
        grad_k.reshape(held_key.shape),
        grad_v.reshape(held_value.shape),
    )


def solution(mesh):
    placed = (
        P("section", "tp", None, None),
        P("section", None, "tp", None),
        P("section", None, "tp", None),
        P("section", None, "tp", None),
    )
    return jax.shard_map(
        local,
        mesh=mesh,
        in_specs=placed,
        out_specs=(
            P("section", None, "tp", None),
            P("section", None, "tp", None),
            P("section", None, "tp", None),
        ),
        check_vma=False,
    )
```
